512 devices in a mesh: outer: 16 (over z_lo, x), inner: 32 (over y, z_hi, core).
Axes of the slice: x: 4, y: 4, z: 16 (z_hi: 4, z_lo: 4; z = z_hi * 4 + z_lo), core: 2. Of those that a mesh axis runs over, the one named last changes fastest.
Arguments:
- image_proj: bfloat16 [65536, 1024], P(('outer', 'inner')), may hold values from -10 to 10
- report_proj: bfloat16 [65536, 1024], P(('outer', 'inner')), may hold values from -10 to 10
- report_feats: bfloat16 [65536, 4096], P(('outer', 'inner')), may hold values from -24 to 24
- pair_index: int32 [65536], P(('outer', 'inner')), may hold values from 0 to 65535, as said below
- natural_log_factor: float32 [1], replicated, may hold values from 1 to 2.3
- logit_bias: float32 [1], replicated, may hold values from -4 to -1
Outputs:
- picture_embedding_grad: bfloat16 [65536, 1024], P(('outer', 'inner'))
- caption_embedding_grad: bfloat16 [65536, 1024], P(('outer', 'inner'))
- head_grad: float32 [4096, 1024], P(('outer', 'inner'))
The draws below stay inside these ranges and needn't reach their ends.
Inputs may be any that keep to these rules, and one draw needn't show every extreme that they name: Within each block of 128 rows, pair_index is a permutation of that block's own global row indices.
All inputs are finite; a program needn't handle non-finite values.
Results may differ from the reference program's by a relative error of at most 0.0058.
Values may be sent and summed in bfloat16 or wider, within the bound.
No kernel may reach another device: no remote copies, remote signals or barrier semaphores. Data moves between devices by JAX's collectives and lax.ppermute only.
A program may use at most 64 MiB of HBM per device.

```python
import jax
import jax.numpy as jnp
from jax import lax

DF = 4096
E = 1024
B_DEV = 128
STEPS = 8
BLOCKS = 512
TOKENS = 65536


def spread_entries(key, entries):
    row_key, col_key = jax.random.split(key)
    count = entries.shape[0]
    width = entries.shape[1]
    row_scale = jnp.exp(jax.random.uniform(row_key, (count, 1), jnp.float32) * 2.302585)
    col_scale = jnp.exp(jax.random.uniform(col_key, (1, width), jnp.float32) * 2.302585)
    return (0.02 * entries * row_scale * col_scale).astype(jnp.bfloat16)


def draw_image_proj(key, part):
    key = jax.random.fold_in(key, 1)
    first, second = jax.random.split(key, 2)
    entries = jax.random.truncated_normal(first, -5.0, 5.0, (TOKENS, E), jnp.float32)
    return spread_entries(second, entries)


def draw_report_proj(key, part):
    key = jax.random.fold_in(key, 2)
    first, second = jax.random.split(key, 2)
    entries = jax.random.truncated_normal(first, -5.0, 5.0, (TOKENS, E), jnp.float32)
    return spread_entries(second, entries)


def draw_pair_index(key, part):
    key = jax.random.fold_in(key, 3)
    block_keys = jax.random.split(key, BLOCKS)
    shuffled = jax.vmap(lambda one_key: jax.random.permutation(one_key, B_DEV))(block_keys)
    starts = jnp.arange(BLOCKS, dtype=jnp.int32)[:, None] * B_DEV
    return (shuffled.astype(jnp.int32) + starts).reshape(TOKENS).astype(jnp.int32)


def raised(array, rng, source, target, shards_of, factor):
    def block_of(position):
        return (jnp.arange(array.shape[position]) // (array.shape[position] // shards_of)).reshape((-1,) + (1,) * (array.ndim - 1 - position))

    one_side = jax.random.permutation(rng, shards_of)[block_of(target)]
    second = (block_of(target) + shards_of // 2) % shards_of
    return jnp.where((block_of(source) == one_side) | (block_of(source) == second), factor * array, array)


def levels(own_key, extent, cuts, smallest, top_value):
    def one(position, parts):
        heights = jax.random.uniform(jax.random.fold_in(jax.random.fold_in(own_key, 6), position), (parts,), jnp.float32, smallest / len(cuts), top_value / len(cuts))
        return jnp.repeat(jnp.exp(heights), extent[position] // parts).reshape((-1,) + (1,) * (len(extent) - position - 1))

    factor_of = one(*cuts[0])
    for cut in cuts[1:]:
        factor_of = factor_of * one(*cut)
    return factor_of


def heavy_noise(key, shape, scale, most, pieces, heavy, kind=jnp.bfloat16):
    array = scale * jax.random.normal(key, shape, jnp.float32)
    if pieces:
        array = array * levels(key, shape, pieces, -0.22, 0.18)
    return jnp.clip(raised(array, jax.random.fold_in(key, 3), *heavy), -most, most).astype(kind)


def setup_inputs(seed: int = 0) -> dict:
    key_of = jax.random.split(jax.random.key(seed), 7)
    image_proj = draw_image_proj(jax.random.fold_in(key_of[6], 71), 0)
    report_proj = draw_report_proj(jax.random.fold_in(key_of[6], 71), 0)
    report_feats = heavy_noise(key_of[2], (TOKENS, DF), 1.0, 24.0, ((0, 512),), (0, 1, 512, 6.0))
    pair_index = draw_pair_index(jax.random.fold_in(key_of[6], 71), 0)
    natural_log_factor = jnp.clip(jax.random.uniform(key_of[4], (1,), jnp.float32, 1.0, 2.3), 1.0, 2.3)
    logit_bias = jnp.clip(jax.random.uniform(key_of[5], (1,), jnp.float32, -4.0, -1.0), -4.0, -1.0)
    return {"image_proj": image_proj, "report_proj": report_proj, "report_feats": report_feats, "pair_index": pair_index, "natural_log_factor": natural_log_factor, "logit_bias": logit_bias}


EPSILON = 1e-06

def unit_rows(values):
    wide = values.astype(jnp.float32)
    length = jnp.sqrt(lax.optimization_barrier(jnp.sum(wide * wide, axis=-1, keepdims=True)) + EPSILON)
    return (wide / length, length)

def euclid_norm_derivative(grad_unit, unit, length):
    return (grad_unit - unit * lax.optimization_barrier(jnp.sum(unit * grad_unit, axis=-1, keepdims=True))) / length

def reference(image_proj, report_proj, report_feats, pair_index, natural_log_factor, logit_bias):
    picture_directions, picture_norms = unit_rows(image_proj)
    caption_directions, caption_norms = unit_rows(report_proj)
    slide_lower_index = lax.optimization_barrier(picture_directions.astype(jnp.bfloat16)).astype(jnp.float32)
    report_low = lax.optimization_barrier(caption_directions.astype(jnp.bfloat16)).astype(jnp.float32)
    picture_tiles = slide_lower_index.reshape(BLOCKS, B_DEV, E)
    report_blocks = report_low.reshape(BLOCKS, B_DEV, E)
    sharpness_factor = jnp.exp(natural_log_factor[0])
    cyclic_offset = logit_bias[0]
    columns = jnp.arange(B_DEV, dtype=jnp.int32)
    pair_cols = (pair_index % B_DEV).astype(jnp.int32).reshape(BLOCKS, B_DEV)
    matching_indicator = pair_cols[:, :, None] == columns[None, None, :]
    picture_energy = jnp.zeros((BLOCKS, B_DEV, E), jnp.float32)
    caption_energy = jnp.zeros((BLOCKS, B_DEV, E), jnp.float32)
    for offset_step in range(STEPS):
        shifted_partner_matrix = jnp.roll(report_blocks, offset_step, axis=0)
        similarity_scores = sharpness_factor * jnp.einsum('zfp,zgp->zfg', picture_tiles, shifted_partner_matrix) + cyclic_offset
        if offset_step == 0:
            target = jnp.where(matching_indicator, 1.0, -1.0).astype(jnp.float32)
        else:
            target = -jnp.ones_like(similarity_scores)
        slope = -target * jax.nn.sigmoid(-target * similarity_scores)
        slope = lax.optimization_barrier(slope.astype(jnp.bfloat16)).astype(jnp.float32)
        picture_energy = picture_energy + jnp.einsum('nac,nce->nae', slope, shifted_partner_matrix)
        term = jnp.einsum('nac,nae->nce', slope, picture_tiles)
        caption_energy = caption_energy + jnp.roll(term, -offset_step, axis=0)
    picture_energy = picture_energy.reshape(TOKENS, E)
    caption_energy = caption_energy.reshape(TOKENS, E)
    picture_embedding_grad = euclid_norm_derivative(sharpness_factor * picture_energy, picture_directions, picture_norms).astype(jnp.bfloat16)
    caption_embedding_grad = euclid_norm_derivative(sharpness_factor * caption_energy, caption_directions, caption_norms).astype(jnp.bfloat16)
    head_grad = lax.dot_general(report_feats.astype(jnp.float32), caption_embedding_grad.astype(jnp.float32), (((0,), (0,)), ((), ())), precision=lax.Precision.HIGHEST)
    return (picture_embedding_grad, caption_embedding_grad, head_grad)
```

```python
import jax
import jax.numpy as jnp
from jax import lax
from jax.experimental import pallas as pl
from jax.experimental.pallas import tpu as pltpu
from jax.sharding import Mesh, PartitionSpec as P

EPSILON = 1e-06
ROWS = 128
WIDTH = 1024
BLOCKS = 512
AXES = ("zl", "x", "y", "zh", "c")
LIMIT = 40 * 1024 * 1024


def moved(value, target_of):
    return lax.ppermute(value, AXES, [(r, target_of(r) % BLOCKS) for r in range(BLOCKS)])


def moved_by(value, steps):
    return moved(value, lambda r: r + steps)


def swapped(value):
    return lax.ppermute(value, "c", [(0, 1), (1, 0)])


def after(value, *others):
    return lax.optimization_barrier((value, *others))[0]


def low_rows(wide):
    inverse = 1.0 / jnp.sqrt(jnp.sum(wide * wide, axis=-1, keepdims=True) + EPSILON)
    return (wide * inverse).astype(jnp.bfloat16)


def window_gradient(scalars, match, own, others, low):
    sharpness = scalars[0]
    offset = scalars[1]
    start = 0
    for ref in others:
        rows = ref.shape[0]
        low[start : start + rows, :] = low_rows(ref[...].astype(jnp.float32))
        start += rows
    wide = own[...].astype(jnp.float32)
    length = jnp.sqrt(jnp.sum(wide * wide, axis=-1, keepdims=True) + EPSILON)
    unit = wide / length
    logits = sharpness * lax.dot_general(
        unit.astype(jnp.bfloat16),
        low[...],
        (((1,), (1,)), ((), ())),
        preferred_element_type=jnp.float32,
    ) + offset
    first = logits[:, :ROWS]
    target = jnp.where(match, 1.0, -1.0)
    first_slope = -target * jax.nn.sigmoid(-target * first)
    slope = jnp.concatenate([first_slope, jax.nn.sigmoid(logits[:, ROWS:])], axis=1)
    total = sharpness * jnp.dot(
        slope.astype(jnp.bfloat16), low[...], preferred_element_type=jnp.float32
    )
    return (total - unit * jnp.sum(unit * total, axis=-1, keepdims=True)) / length


def caption_kernel(scalars, pair_row, own, *refs):
    *others, out, spread, low = refs
    rows = lax.broadcasted_iota(jnp.int32, (ROWS, ROWS), 0)
    match = rows == lax.rem(pair_row[...], ROWS)
    grad = window_gradient(scalars, match, own, others, low).astype(jnp.bfloat16)
    out[...] = grad
    for x in range(4):
        for y in range(4):
            spread[x, y] = grad[:, y * 256 : (y + 1) * 256]


def picture_kernel(scalars, pair_column, own, *refs):
    *others, out, low = refs
    columns = lax.broadcasted_iota(jnp.int32, (ROWS, ROWS), 1)
    match = columns == lax.rem(pair_column[...], ROWS)
    out[...] = window_gradient(scalars, match, own, others, low).astype(jnp.bfloat16)


def window_call(body, outs, *args):
    return pl.pallas_call(
        body,
        out_shape=outs,
        in_specs=[pl.BlockSpec(memory_space=pltpu.SMEM)]
        + [pl.BlockSpec(memory_space=pltpu.VMEM)] * (len(args) - 1),
        out_specs=jax.tree.map(lambda _: pl.BlockSpec(memory_space=pltpu.VMEM), outs),
        scratch_shapes=[pltpu.VMEM((8 * ROWS, WIDTH), jnp.bfloat16)],
        compiler_params=pltpu.CompilerParams(vmem_limit_bytes=LIMIT),
        cost_estimate=pl.CostEstimate(
            flops=4 * ROWS * 8 * ROWS * WIDTH, bytes_accessed=4_000_000, transcendentals=ROWS * 1024
        ),
    )(*args)


def head_kernel(place, caps, f0, f1, f2, f3, keep, give, table):
    y = place[0]
    c = place[1]
    total = None
    for step, feats in enumerate((f0, f1, f2, f3)):
        source = lax.rem(y + 4 - step, 4)
        rows = jnp.concatenate([caps[x, source] for x in range(4)], axis=0)
        part = lax.dot_general(
            rows, feats[...], (((0,), (0,)), ((), ())), preferred_element_type=jnp.float32
        )
        total = part if total is None else total + part
    table[...] = total.T
    for zl in range(4):
        for zh in range(4):
            for yy in range(4):
                base = zl * 256 + yy * 64 + zh * 16
                to = (zl * 16 + zh * 4 + yy) * 8
                keep[to : to + 8, :] = table[pl.ds(pl.multiple_of(base + c * 8, 8), 8), :]
                give[to : to + 8, :] = table[pl.ds(pl.multiple_of(base + 8 - c * 8, 8), 8), :]


def head_call(place, caps, feats):
    vmem = pl.BlockSpec(memory_space=pltpu.VMEM)
    half = jax.ShapeDtypeStruct((512, 256), jnp.float32)
    return pl.pallas_call(
        head_kernel,
        out_shape=(half, half),
        in_specs=[pl.BlockSpec(memory_space=pltpu.SMEM)] + [vmem] * 5,
        out_specs=(vmem, vmem),
        scratch_shapes=[pltpu.VMEM((1024, 256), jnp.float32)],
        compiler_params=pltpu.CompilerParams(vmem_limit_bytes=LIMIT),
        cost_estimate=pl.CostEstimate(
            flops=2 * 2048 * 1024 * 256, bytes_accessed=6_000_000, transcendentals=0
        ),
    )(place, caps, *feats)


def on_device(image_proj, report_proj, report_feats, pair_index, natural_log_factor, logit_bias):
    scalars = jnp.concatenate([jnp.exp(natural_log_factor), logit_bias])
    place = jnp.stack([lax.axis_index("y"), lax.axis_index("c")]).astype(jnp.int32)

    image_beside = moved(image_proj, lambda r: r - 1 if r % 2 else r - 7)
    image_1 = moved_by(image_proj, -2)
    image_3 = moved_by(image_proj, -6)

    ordered = report_feats.reshape(ROWS, 4, 4, 256).transpose(2, 0, 1, 3).reshape(512, 1024)
    columns = lax.all_to_all(ordered, "x", split_axis=0, concat_axis=0, tiled=True)
    feats = [columns] + [
        lax.ppermute(columns, "y", [(i, (i + k) % 4) for i in range(4)]) for k in (1, 2, 3)
    ]

    image_2a = moved_by(image_1[:64], -2)
    image_2b = moved_by(image_3[64:], 2)
    images = (image_proj, image_beside, image_1, swapped(image_1), image_3, swapped(image_3))
    images += (image_2a, image_2b, swapped(image_2a), swapped(image_2b))
    caption_grad, caption_spread = window_call(
        caption_kernel,
        (
            jax.ShapeDtypeStruct((ROWS, WIDTH), jnp.bfloat16),
            jax.ShapeDtypeStruct((4, 4, ROWS, 256), jnp.bfloat16),
        ),
        scalars,
        pair_index.reshape(1, ROWS),
        report_proj,
        *images,
    )

    report_late = after(report_proj, image_2a, image_2b)
    report_beside = moved(report_late, lambda r: r + 7 if r % 2 else r + 1)
    report_1 = moved_by(report_late, 2)
    report_3 = moved_by(report_late, 6)
    report_2a = moved_by(report_1[:64], 2)
    report_2b = moved_by(report_3[64:], -2)
    reports = (report_proj, report_beside, report_1, swapped(report_1), report_3, swapped(report_3))
    reports += (report_2a, report_2b, swapped(report_2a), swapped(report_2b))
    picture_grad = window_call(
        picture_kernel,
        jax.ShapeDtypeStruct((ROWS, WIDTH), jnp.bfloat16),
        scalars,
        pair_index.reshape(ROWS, 1),
        image_proj,
        *reports,
    )

    caps = lax.all_to_all(
        caption_spread.reshape(16 * ROWS, 256), ("x", "y"), split_axis=0, concat_axis=0, tiled=True
    ).reshape(4, 4, ROWS, 256)
    keep, give = head_call(place, caps, feats)
    part = (keep + swapped(give)).astype(jnp.bfloat16)
    parts = lax.all_to_all(part, ("zl", "zh", "y"), split_axis=0, concat_axis=0, tiled=True)
    head = jnp.sum(parts.reshape(16, 4, 8, 256).astype(jnp.float32), axis=0)
    head_grad = head.transpose(1, 0, 2).reshape(8, WIDTH)
    return (picture_grad, caption_grad, head_grad)


def solution(mesh):
    fine = Mesh(mesh.devices.reshape(4, 4, 4, 4, 2), AXES)
    rows = P(AXES, None)
    return jax.shard_map(
        on_device,
        mesh=fine,
        in_specs=(rows, rows, rows, P(AXES), P(), P()),
        out_specs=(rows, rows, rows),
        check_vma=False,
    )
```

```python
import jax
import jax.numpy as jnp
from jax import lax
from jax.experimental import pallas as pl
from jax.experimental.pallas import tpu as pltpu
from jax.sharding import Mesh, PartitionSpec as P

EPSILON = 1e-06
ROWS = 128
WIDTH = 1024
BLOCKS = 512
AXES = ("zl", "x", "y", "zh", "c")
LIMIT = 40 * 1024 * 1024
WINDOW_FLOPS = 4 * ROWS * 8 * ROWS * WIDTH
CAPTION_FLOPS = 70 * WINDOW_FLOPS
READY_FLOPS = 60 * WINDOW_FLOPS
PICTURE_FLOPS = 1 * WINDOW_FLOPS
HEAD_FLOPS = 2 * 2048 * 1024 * 256


def moved(value, target_of):
    return lax.ppermute(value, AXES, [(r, target_of(r) % BLOCKS) for r in range(BLOCKS)])


def moved_by(value, steps):
    return moved(value, lambda r: r + steps)


def swapped(value):
    return lax.ppermute(value, "c", [(0, 1), (1, 0)])


def after(value, *others):
    return lax.optimization_barrier((value, *others))[0]


def low_rows(wide):
    inverse = 1.0 / jnp.sqrt(jnp.sum(wide * wide, axis=-1, keepdims=True) + EPSILON)
    return (wide * inverse).astype(jnp.bfloat16)


def window_gradient(scalars, match, own, others, low):
    sharpness = scalars[0]
    offset = scalars[1]
    start = 0
    for ref in others:
        rows = ref.shape[0]
        low[start : start + rows, :] = low_rows(ref[...].astype(jnp.float32))
        start += rows
    wide = own[...].astype(jnp.float32)
    length = jnp.sqrt(jnp.sum(wide * wide, axis=-1, keepdims=True) + EPSILON)
    unit = wide / length
    logits = sharpness * lax.dot_general(
        unit.astype(jnp.bfloat16),
        low[...],
        (((1,), (1,)), ((), ())),
        preferred_element_type=jnp.float32,
    ) + offset
    first = logits[:, :ROWS]
    target = jnp.where(match, 1.0, -1.0)
    first_slope = -target * jax.nn.sigmoid(-target * first)
    slope = jnp.concatenate([first_slope, jax.nn.sigmoid(logits[:, ROWS:])], axis=1)
    total = sharpness * jnp.dot(
        slope.astype(jnp.bfloat16), low[...], preferred_element_type=jnp.float32
    )
    return (total - unit * jnp.sum(unit * total, axis=-1, keepdims=True)) / length


def caption_kernel(scalars, pair_row, own, *refs):
    *others, out, spread, low = refs
    rows = lax.broadcasted_iota(jnp.int32, (ROWS, ROWS), 0)
    match = rows == lax.rem(pair_row[...], ROWS)
    grad = window_gradient(scalars, match, own, others, low).astype(jnp.bfloat16)
    out[...] = grad
    for x in range(4):
        for y in range(4):
            spread[x, y] = grad[:, y * 256 : (y + 1) * 256]


def picture_kernel(scalars, pair_column, own, *refs):
    *others, out, low = refs
    columns = lax.broadcasted_iota(jnp.int32, (ROWS, ROWS), 1)
    match = columns == lax.rem(pair_column[...], ROWS)
    out[...] = window_gradient(scalars, match, own, others, low).astype(jnp.bfloat16)


def window_call(body, outs, flops, *args):
    return pl.pallas_call(
        body,
        out_shape=outs,
        in_specs=[pl.BlockSpec(memory_space=pltpu.SMEM)]
        + [pl.BlockSpec(memory_space=pltpu.VMEM)] * (len(args) - 1),
        out_specs=jax.tree.map(lambda _: pl.BlockSpec(memory_space=pltpu.VMEM), outs),
        scratch_shapes=[pltpu.VMEM((8 * ROWS, WIDTH), jnp.bfloat16)],
        compiler_params=pltpu.CompilerParams(vmem_limit_bytes=LIMIT),
        cost_estimate=pl.CostEstimate(
            flops=flops, bytes_accessed=4_000_000, transcendentals=ROWS * 1024
        ),
    )(*args)


def head_kernel(place, caps, feats, arrived, keep, give, table):
    c = place[0]
    total = lax.dot_general(
        caps[...], feats[...], (((0,), (0,)), ((), ())), preferred_element_type=jnp.float32
    )
    table[...] = total.T
    for zl in range(4):
        for zh in range(4):
            for y in range(4):
                base = zl * 256 + y * 64 + zh * 16
                to = (zl * 16 + zh * 4 + y) * 8
                keep[to : to + 8, :] = table[pl.ds(pl.multiple_of(base + c * 8, 8), 8), :]
                give[to : to + 8, :] = table[pl.ds(pl.multiple_of(base + 8 - c * 8, 8), 8), :]


def head_call(place, caps, feats, arrived):
    vmem = pl.BlockSpec(memory_space=pltpu.VMEM)
    half = jax.ShapeDtypeStruct((512, 256), jnp.float32)
    return pl.pallas_call(
        head_kernel,
        out_shape=(half, half),
        in_specs=[pl.BlockSpec(memory_space=pltpu.SMEM)] + [vmem] * 3,
        out_specs=(vmem, vmem),
        scratch_shapes=[pltpu.VMEM((1024, 256), jnp.float32)],
        compiler_params=pltpu.CompilerParams(vmem_limit_bytes=LIMIT),
        cost_estimate=pl.CostEstimate(
            flops=HEAD_FLOPS, bytes_accessed=6_000_000, transcendentals=0
        ),
    )(place, caps, feats, arrived)


def ready_kernel(first, second, out):
    out[...] = first[...].astype(jnp.float32) + second[...].astype(jnp.float32)


def ready(first, second):
    return pl.pallas_call(
        ready_kernel,
        grid=(1,),
        out_shape=jax.ShapeDtypeStruct((16, 128), jnp.float32),
        in_specs=[pl.BlockSpec((16, 128), lambda i: (0, 0))] * 2,
        out_specs=pl.BlockSpec((16, 128), lambda i: (0, 0)),
        cost_estimate=pl.CostEstimate(flops=READY_FLOPS, bytes_accessed=16384, transcendentals=0),
    )(first, second)


def on_device(image_proj, report_proj, report_feats, pair_index, natural_log_factor, logit_bias):
    scalars = jnp.concatenate([jnp.exp(natural_log_factor), logit_bias])
    place = lax.axis_index("c").astype(jnp.int32).reshape(1)

    with jax.named_scope("image_near"):
        image_1 = moved_by(image_proj, -2)
    with jax.named_scope("image_far"):
        image_3 = moved_by(image_proj, -6)
    with jax.named_scope("image_beside"):
        image_beside = moved(image_proj, lambda r: r - 1 if r % 2 else r - 7)

    with jax.named_scope("feats"):
        ordered = report_feats.reshape(ROWS, 4, 4, 256).transpose(2, 0, 1, 3)
        ordered = jnp.broadcast_to(ordered[:, None], (4, 4, ROWS, 4, 256)).reshape(16 * ROWS, WIDTH)
        feats = lax.all_to_all(ordered, ("x", "y"), split_axis=0, concat_axis=0, tiled=True)

    with jax.named_scope("image_relay_near"):
        image_2a = moved_by(image_1[:64], -2)
    with jax.named_scope("image_relay_far"):
        image_2b = moved_by(image_3[64:], 2)
    with jax.named_scope("image_swap"):
        images = (image_proj, image_beside, image_1, swapped(image_1), image_3, swapped(image_3))
        images += (image_2a, image_2b, swapped(image_2a), swapped(image_2b))
    with jax.named_scope("caption_kernel"):
        caption_grad, caption_spread = window_call(
            caption_kernel,
            (
                jax.ShapeDtypeStruct((ROWS, WIDTH), jnp.bfloat16),
                jax.ShapeDtypeStruct((4, 4, ROWS, 256), jnp.bfloat16),
            ),
            CAPTION_FLOPS,
            scalars,
            pair_index.reshape(1, ROWS),
            report_proj,
            *images,
        )

    report_late = after(report_proj, image_2a, image_2b)
    with jax.named_scope("report_near"):
        report_1 = moved_by(report_late, 2)
    with jax.named_scope("report_far"):
        report_3 = moved_by(report_late, 6)
    with jax.named_scope("report_beside"):
        report_beside = moved(report_late, lambda r: r + 7 if r % 2 else r + 1)
    with jax.named_scope("report_relay_near"):
        report_2a = moved_by(report_1[:64], 2)
    with jax.named_scope("report_relay_far"):
        report_2b = moved_by(report_3[64:], -2)
    with jax.named_scope("report_swap"):
        report_1s = swapped(report_1)
        report_3s = swapped(report_3)
        reports = (report_proj, report_beside, report_1, report_1s, report_3, report_3s)
        reports += (report_2a, report_2b, swapped(report_2a), swapped(report_2b))
    with jax.named_scope("picture_kernel"):
        picture_grad = window_call(
            picture_kernel,
            jax.ShapeDtypeStruct((ROWS, WIDTH), jnp.bfloat16),
            PICTURE_FLOPS,
            scalars,
            pair_index.reshape(ROWS, 1),
            image_proj,
            *reports,
        )

    with jax.named_scope("captions"):
        caps = lax.all_to_all(
            after(caption_spread, feats).reshape(16 * ROWS, 256),
            ("x", "y"),
            split_axis=0,
            concat_axis=0,
            tiled=True,
        )
    with jax.named_scope("head_kernel"):
        keep, give = head_call(place, caps, feats, ready(report_1, report_3))
    with jax.named_scope("head_swap"):
        part = (keep + swapped(give)).astype(jnp.bfloat16)
    with jax.named_scope("head_sum"):
        parts = lax.all_to_all(part, ("zl", "zh", "y"), split_axis=0, concat_axis=0, tiled=True)
        head = jnp.sum(parts.reshape(16, 4, 8, 256).astype(jnp.float32), axis=0)
        head_grad = head.transpose(1, 0, 2).reshape(8, WIDTH)
    return (picture_grad, caption_grad, head_grad)


def solution(mesh):
    fine = Mesh(mesh.devices.reshape(4, 4, 4, 4, 2), AXES)
    rows = P(AXES, None)
    return jax.shard_map(
        on_device,
        mesh=fine,
        in_specs=(rows, rows, rows, P(AXES), P(), P()),
        out_specs=(rows, rows, rows),
        check_vma=False,
    )
```

```python
import jax
import jax.numpy as jnp
from jax import lax
from jax.experimental import pallas as pl
from jax.experimental.pallas import tpu as pltpu
from jax.sharding import Mesh, PartitionSpec as P

EPSILON = 1e-06
ROWS = 128
WIDTH = 1024
BLOCKS = 512
AXES = ("zl", "x", "y", "zh", "c")
LIMIT = 40 * 1024 * 1024
WINDOW_FLOPS = 4 * ROWS * 8 * ROWS * WIDTH
CAPTION_FLOPS = 70 * WINDOW_FLOPS
READY_FLOPS = 14 * WINDOW_FLOPS
PICTURE_FLOPS = 1 * WINDOW_FLOPS
HEAD_FLOPS = 2 * 2048 * 1024 * 256


def moved(value, target_of):
    return lax.ppermute(value, AXES, [(r, target_of(r) % BLOCKS) for r in range(BLOCKS)])


def moved_by(value, steps):
    return moved(value, lambda r: r + steps)


def swapped(value):
    return lax.ppermute(value, "c", [(0, 1), (1, 0)])


def after(value, *others):
    return lax.optimization_barrier((value, *others))[0]


def low_rows(wide):
    inverse = 1.0 / jnp.sqrt(jnp.sum(wide * wide, axis=-1, keepdims=True) + EPSILON)
    return (wide * inverse).astype(jnp.bfloat16)


def window_gradient(scalars, match, own, others, low):
    sharpness = scalars[0]
    offset = scalars[1]
    start = 0
    for ref in others:
        rows = ref.shape[0]
        low[start : start + rows, :] = low_rows(ref[...].astype(jnp.float32))
        start += rows
    wide = own[...].astype(jnp.float32)
    length = jnp.sqrt(jnp.sum(wide * wide, axis=-1, keepdims=True) + EPSILON)
    unit = wide / length
    logits = sharpness * lax.dot_general(
        unit.astype(jnp.bfloat16),
        low[...],
        (((1,), (1,)), ((), ())),
        preferred_element_type=jnp.float32,
    ) + offset
    first = logits[:, :ROWS]
    target = jnp.where(match, 1.0, -1.0)
    first_slope = -target * jax.nn.sigmoid(-target * first)
    slope = jnp.concatenate([first_slope, jax.nn.sigmoid(logits[:, ROWS:])], axis=1)
    total = sharpness * jnp.dot(
        slope.astype(jnp.bfloat16), low[...], preferred_element_type=jnp.float32
    )
    return (total - unit * jnp.sum(unit * total, axis=-1, keepdims=True)) / length


def caption_kernel(scalars, pair_row, own, *refs):
    *others, out, spread, low = refs
    rows = lax.broadcasted_iota(jnp.int32, (ROWS, ROWS), 0)
    match = rows == lax.rem(pair_row[...], ROWS)
    grad = window_gradient(scalars, match, own, others, low).astype(jnp.bfloat16)
    out[...] = grad
    for x in range(4):
        for y in range(4):
            spread[x, y] = grad[:, y * 256 : (y + 1) * 256]


def picture_kernel(scalars, pair_column, own, *refs):
    *others, out, low = refs
    columns = lax.broadcasted_iota(jnp.int32, (ROWS, ROWS), 1)
    match = columns == lax.rem(pair_column[...], ROWS)
    out[...] = window_gradient(scalars, match, own, others, low).astype(jnp.bfloat16)


def window_call(body, outs, flops, *args):
    return pl.pallas_call(
        body,
        out_shape=outs,
        in_specs=[pl.BlockSpec(memory_space=pltpu.SMEM)]
        + [pl.BlockSpec(memory_space=pltpu.VMEM)] * (len(args) - 1),
        out_specs=jax.tree.map(lambda _: pl.BlockSpec(memory_space=pltpu.VMEM), outs),
        scratch_shapes=[pltpu.VMEM((8 * ROWS, WIDTH), jnp.bfloat16)],
        compiler_params=pltpu.CompilerParams(vmem_limit_bytes=LIMIT),
        cost_estimate=pl.CostEstimate(
            flops=flops, bytes_accessed=4_000_000, transcendentals=ROWS * 1024
        ),
    )(*args)


def head_kernel(place, caps, feats, arrived, keep, give, table):
    c = place[0]
    total = lax.dot_general(
        caps[...], feats[...], (((0,), (0,)), ((), ())), preferred_element_type=jnp.float32
    )
    table[...] = total.T
    for zl in range(4):
        for zh in range(4):
            for y in range(4):
                base = zl * 256 + y * 64 + zh * 16
                to = (zl * 16 + zh * 4 + y) * 8
                keep[to : to + 8, :] = table[pl.ds(pl.multiple_of(base + c * 8, 8), 8), :]
                give[to : to + 8, :] = table[pl.ds(pl.multiple_of(base + 8 - c * 8, 8), 8), :]


def head_call(place, caps, feats, arrived):
    vmem = pl.BlockSpec(memory_space=pltpu.VMEM)
    half = jax.ShapeDtypeStruct((512, 256), jnp.float32)
    return pl.pallas_call(
        head_kernel,
        out_shape=(half, half),
        in_specs=[pl.BlockSpec(memory_space=pltpu.SMEM)] + [vmem] * 3,
        out_specs=(vmem, vmem),
        scratch_shapes=[pltpu.VMEM((1024, 256), jnp.float32)],
        compiler_params=pltpu.CompilerParams(vmem_limit_bytes=LIMIT),
        cost_estimate=pl.CostEstimate(
            flops=HEAD_FLOPS, bytes_accessed=6_000_000, transcendentals=0
        ),
    )(place, caps, feats, arrived)


def columns_kernel(feats, out):
    for x in range(4):
        for zl in range(4):
            piece = feats[:, zl * 1024 + x * 256 : zl * 1024 + x * 256 + 256]
            for y in range(4):
                row = (x * 4 + y) * ROWS
                out[row : row + ROWS, zl * 256 : zl * 256 + 256] = piece


def columns_call(feats):
    vmem = pl.BlockSpec(memory_space=pltpu.VMEM)
    return pl.pallas_call(
        columns_kernel,
        out_shape=jax.ShapeDtypeStruct((16 * ROWS, WIDTH), jnp.bfloat16),
        in_specs=[vmem],
        out_specs=vmem,
        compiler_params=pltpu.CompilerParams(vmem_limit_bytes=LIMIT),
        cost_estimate=pl.CostEstimate(flops=0, bytes_accessed=5_000_000, transcendentals=0),
    )(feats)


def ready_kernel(first, second, out):
    out[...] = first[...].astype(jnp.float32) + second[...].astype(jnp.float32)


def ready(first, second):
    return pl.pallas_call(
        ready_kernel,
        grid=(1,),
        out_shape=jax.ShapeDtypeStruct((16, 128), jnp.float32),
        in_specs=[pl.BlockSpec((16, 128), lambda i: (0, 0))] * 2,
        out_specs=pl.BlockSpec((16, 128), lambda i: (0, 0)),
        cost_estimate=pl.CostEstimate(flops=READY_FLOPS, bytes_accessed=16384, transcendentals=0),
    )(first, second)


def on_device(image_proj, report_proj, report_feats, pair_index, natural_log_factor, logit_bias):
    scalars = jnp.concatenate([jnp.exp(natural_log_factor), logit_bias])
    place = lax.axis_index("c").astype(jnp.int32).reshape(1)

    with jax.named_scope("image_near"):
        image_1 = moved_by(image_proj, -2)
    with jax.named_scope("image_far"):
        image_3 = moved_by(image_proj, -6)
    with jax.named_scope("image_beside"):
        image_beside = moved(image_proj, lambda r: r - 1 if r % 2 else r - 7)

    with jax.named_scope("feats"):
        ordered = columns_call(after(report_feats, image_beside))
        feats = lax.all_to_all(ordered, ("x", "y"), split_axis=0, concat_axis=0, tiled=True)

    with jax.named_scope("image_relay_near"):
        image_2a = moved_by(image_1[:64], -2)
    with jax.named_scope("image_relay_far"):
        image_2b = moved_by(image_3[64:], 2)
    with jax.named_scope("image_swap"):
        images = (image_proj, image_beside, image_1, swapped(image_1), image_3, swapped(image_3))
        images += (image_2a, image_2b, swapped(image_2a), swapped(image_2b))
    with jax.named_scope("caption_kernel"):
        caption_grad, caption_spread = window_call(
            caption_kernel,
            (
                jax.ShapeDtypeStruct((ROWS, WIDTH), jnp.bfloat16),
                jax.ShapeDtypeStruct((4, 4, ROWS, 256), jnp.bfloat16),
            ),
            CAPTION_FLOPS,
            scalars,
            pair_index.reshape(1, ROWS),
            report_proj,
            *images,
        )

    report_late = after(report_proj, image_2a, image_2b)
    with jax.named_scope("report_near"):
        report_1 = moved_by(report_late, 2)
    with jax.named_scope("report_far"):
        report_3 = moved_by(report_late, 6)
    with jax.named_scope("report_beside"):
        report_beside = moved(report_late, lambda r: r + 7 if r % 2 else r + 1)
    with jax.named_scope("report_relay_near"):
        report_2a = moved_by(report_1[:64], 2)
    with jax.named_scope("report_relay_far"):
        report_2b = moved_by(report_3[64:], -2)
    with jax.named_scope("report_swap"):
        report_1s = swapped(report_1)
        report_3s = swapped(report_3)
        reports = (report_proj, report_beside, report_1, report_1s, report_3, report_3s)
        reports += (report_2a, report_2b, swapped(report_2a), swapped(report_2b))
    with jax.named_scope("picture_kernel"):
        picture_grad = window_call(
            picture_kernel,
            jax.ShapeDtypeStruct((ROWS, WIDTH), jnp.bfloat16),
            PICTURE_FLOPS,
            scalars,
            pair_index.reshape(ROWS, 1),
            image_proj,
            *reports,
        )

    with jax.named_scope("captions"):
        caps = lax.all_to_all(
            after(caption_spread, feats).reshape(16 * ROWS, 256),
            ("x", "y"),
            split_axis=0,
            concat_axis=0,
            tiled=True,
        )
    with jax.named_scope("head_kernel"):
        keep, give = head_call(place, caps, feats, ready(report_2a, report_2b))
    with jax.named_scope("head_swap"):
        part = (keep + swapped(give)).astype(jnp.bfloat16)
    with jax.named_scope("head_sum"):
        parts = lax.all_to_all(part, ("zl", "zh", "y"), split_axis=0, concat_axis=0, tiled=True)
        head = jnp.sum(parts.reshape(16, 4, 8, 256).astype(jnp.float32), axis=0)
        head_grad = head.transpose(1, 0, 2).reshape(8, WIDTH)
    return (picture_grad, caption_grad, head_grad)


def solution(mesh):
    fine = Mesh(mesh.devices.reshape(4, 4, 4, 4, 2), AXES)
    rows = P(AXES, None)
    return jax.shard_map(
        on_device,
        mesh=fine,
        in_specs=(rows, rows, rows, P(AXES), P(), P()),
        out_specs=(rows, rows, rows),
        check_vma=False,
    )
```

```python
import jax
import jax.numpy as jnp
from jax import lax
from jax.experimental import pallas as pl
from jax.experimental.pallas import tpu as pltpu
from jax.sharding import Mesh, PartitionSpec as P

EPSILON = 1e-06
ROWS = 128
WIDTH = 1024
BLOCKS = 512
AXES = ("zl", "x", "y", "zh", "c")
LIMIT = 40 * 1024 * 1024
WINDOW_FLOPS = 4 * ROWS * 8 * ROWS * WIDTH
CAPTION_FLOPS = 65 * WINDOW_FLOPS
PICTURE_FLOPS = 1 * WINDOW_FLOPS
HEAD_FLOPS = 2 * 2048 * 1024 * 256


def moved(value, target_of):
    return lax.ppermute(value, AXES, [(r, target_of(r) % BLOCKS) for r in range(BLOCKS)])


def moved_by(value, steps):
    return moved(value, lambda r: r + steps)


def swapped(value):
    return lax.ppermute(value, "c", [(0, 1), (1, 0)])


def beside(value, parity, steps):
    pairs = [(r, (r + steps) % BLOCKS) for r in range(parity, BLOCKS, 2)]
    return lax.ppermute(value, AXES, pairs)


def after(value, *others):
    return lax.optimization_barrier((value, *others))[0]


def low_rows(wide):
    inverse = 1.0 / jnp.sqrt(jnp.sum(wide * wide, axis=-1, keepdims=True) + EPSILON)
    return (wide * inverse).astype(jnp.bfloat16)


def unit_rows(own):
    wide = own[...].astype(jnp.float32)
    length = jnp.sqrt(jnp.sum(wide * wide, axis=-1, keepdims=True) + EPSILON)
    return wide / length, length


def slopes(scalars, rows, blocks):
    logits = lax.dot_general(
        rows.astype(jnp.bfloat16), blocks, (((1,), (1,)), ((), ())), preferred_element_type=jnp.float32
    )
    return scalars[0] * logits + scalars[1]


def window_sums(scalars, match, use_beside, own, other, blocks, beside, mine, theirs, low):
    start = 0
    for ref in blocks:
        rows = ref.shape[0]
        low[start : start + rows, :] = low_rows(ref[...].astype(jnp.float32))
        start += rows
    last = jnp.where(use_beside, beside[...].astype(jnp.float32), blocks[0][...].astype(jnp.float32))
    low[start : start + ROWS, :] = low_rows(last)
    unit, _ = unit_rows(own)
    logits = slopes(scalars, unit, low[:512, :])
    target = jnp.where(match, 1.0, -1.0)
    first = -target * jax.nn.sigmoid(-target * logits[:, :ROWS])
    slope = jnp.concatenate([first, jax.nn.sigmoid(logits[:, ROWS:])], axis=1)
    mine[...] = jnp.dot(
        slope.astype(jnp.bfloat16), low[:512, :], preferred_element_type=jnp.float32
    )
    unit, _ = unit_rows(other)
    slope = jax.nn.sigmoid(slopes(scalars, unit, low[ROWS:, :]))
    theirs[...] = jnp.dot(
        slope.astype(jnp.bfloat16), low[ROWS:, :], preferred_element_type=jnp.float32
    )


def caption_kernel(scalars, place, pair_row, own, other, *refs):
    *blocks, beside, mine, theirs, low = refs
    rows = lax.broadcasted_iota(jnp.int32, (ROWS, ROWS), 0)
    match = rows == lax.rem(pair_row[...], ROWS)
    window_sums(scalars, match, place[0] == 0, own, other, blocks, beside, mine, theirs, low)


def picture_kernel(scalars, place, pair_column, own, other, *refs):
    *blocks, beside, mine, theirs, low = refs
    columns = lax.broadcasted_iota(jnp.int32, (ROWS, ROWS), 1)
    match = columns == lax.rem(pair_column[...], ROWS)
    window_sums(scalars, match, place[0] == 1, own, other, blocks, beside, mine, theirs, low)


def window_call(body, flops, *args):
    vmem = pl.BlockSpec(memory_space=pltpu.VMEM)
    half = jax.ShapeDtypeStruct((ROWS, WIDTH), jnp.float32)
    return pl.pallas_call(
        body,
        out_shape=(half, half),
        in_specs=[pl.BlockSpec(memory_space=pltpu.SMEM)] * 2 + [vmem] * (len(args) - 2),
        out_specs=(vmem, vmem),
        scratch_shapes=[pltpu.VMEM((5 * ROWS, WIDTH), jnp.bfloat16)],
        compiler_params=pltpu.CompilerParams(vmem_limit_bytes=LIMIT),
        cost_estimate=pl.CostEstimate(
            flops=flops, bytes_accessed=4_000_000, transcendentals=ROWS * 1024
        ),
    )(*args)


def finish_kernel(scalars, own, mine, received, out, *spread):
    unit, length = unit_rows(own)
    total = scalars[0] * (mine[...] + received[...])
    grad = (total - unit * jnp.sum(unit * total, axis=-1, keepdims=True)) / length
    grad = grad.astype(jnp.bfloat16)
    out[...] = grad
    for ref in spread:
        for x in range(4):
            for y in range(4):
                row = (x * 4 + y) * ROWS
                ref[row : row + ROWS, :] = grad[:, y * 256 : (y + 1) * 256]


def finish_call(outs, *args):
    vmem = pl.BlockSpec(memory_space=pltpu.VMEM)
    return pl.pallas_call(
        finish_kernel,
        out_shape=outs,
        in_specs=[pl.BlockSpec(memory_space=pltpu.SMEM)] + [vmem] * 3,
        out_specs=tuple([vmem] * len(outs)),
        compiler_params=pltpu.CompilerParams(vmem_limit_bytes=LIMIT),
        cost_estimate=pl.CostEstimate(flops=0, bytes_accessed=1_500_000, transcendentals=0),
    )(*args)


def head_kernel(place, caps, feats, keep, give, table):
    c = place[0]
    total = lax.dot_general(
        caps[...], feats[...], (((0,), (0,)), ((), ())), preferred_element_type=jnp.float32
    )
    table[...] = total.T
    for zl in range(4):
        for zh in range(4):
            for y in range(4):
                base = zl * 256 + y * 64 + zh * 16
                to = (zl * 16 + zh * 4 + y) * 8
                keep[to : to + 8, :] = table[pl.ds(pl.multiple_of(base + c * 8, 8), 8), :]
                give[to : to + 8, :] = table[pl.ds(pl.multiple_of(base + 8 - c * 8, 8), 8), :]


def head_call(place, caps, feats):
    vmem = pl.BlockSpec(memory_space=pltpu.VMEM)
    half = jax.ShapeDtypeStruct((512, 256), jnp.float32)
    return pl.pallas_call(
        head_kernel,
        out_shape=(half, half),
        in_specs=[pl.BlockSpec(memory_space=pltpu.SMEM)] + [vmem] * 2,
        out_specs=(vmem, vmem),
        scratch_shapes=[pltpu.VMEM((1024, 256), jnp.float32)],
        compiler_params=pltpu.CompilerParams(vmem_limit_bytes=LIMIT),
        cost_estimate=pl.CostEstimate(
            flops=HEAD_FLOPS, bytes_accessed=6_000_000, transcendentals=0
        ),
    )(place, caps, feats)


def columns_kernel(feats, out):
    for x in range(4):
        for zl in range(4):
            piece = feats[:, zl * 1024 + x * 256 : zl * 1024 + x * 256 + 256]
            for y in range(4):
                row = (x * 4 + y) * ROWS
                out[row : row + ROWS, zl * 256 : zl * 256 + 256] = piece


def columns_call(feats):
    vmem = pl.BlockSpec(memory_space=pltpu.VMEM)
    return pl.pallas_call(
        columns_kernel,
        out_shape=jax.ShapeDtypeStruct((16 * ROWS, WIDTH), jnp.bfloat16),
        in_specs=[vmem],
        out_specs=vmem,
        compiler_params=pltpu.CompilerParams(vmem_limit_bytes=LIMIT),
        cost_estimate=pl.CostEstimate(flops=0, bytes_accessed=5_000_000, transcendentals=0),
    )(feats)


def on_device(image_proj, report_proj, report_feats, pair_index, natural_log_factor, logit_bias):
    scalars = jnp.concatenate([jnp.exp(natural_log_factor), logit_bias])
    place = lax.axis_index("c").astype(jnp.int32).reshape(1)

    with jax.named_scope("image_near"):
        image_1 = moved_by(image_proj, -2)
    with jax.named_scope("image_far"):
        image_3 = moved_by(image_proj, -6)
    with jax.named_scope("image_beside"):
        image_beside = beside(image_proj, 0, -8)
    with jax.named_scope("core_swap"):
        image_other = swapped(image_proj)
        report_other = after(swapped(report_proj), image_other)

    with jax.named_scope("feats"):
        feats = lax.all_to_all(
            columns_call(report_feats), ("x", "y"), split_axis=0, concat_axis=0, tiled=True
        )

    with jax.named_scope("image_relay_near"):
        image_2a = moved_by(image_1[:64], -2)
    with jax.named_scope("image_relay_far"):
        image_2b = moved_by(image_3[64:], 2)
    with jax.named_scope("caption_kernel"):
        caption_mine, caption_theirs = window_call(
            caption_kernel,
            CAPTION_FLOPS,
            scalars,
            place,
            pair_index.reshape(1, ROWS),
            report_proj,
            report_other,
            image_proj,
            image_1,
            image_2a,
            image_2b,
            image_3,
            image_beside,
        )
    report_late = after(report_proj, image_1, image_3)
    with jax.named_scope("report_near"):
        report_1 = moved_by(report_late, 2)
    with jax.named_scope("report_far"):
        report_3 = moved_by(report_late, 6)
    with jax.named_scope("caption_swap"):
        caption_received = swapped(after(caption_theirs, report_1, report_3))
    with jax.named_scope("caption_finish"):
        caption_grad, caption_spread = finish_call(
            (
                jax.ShapeDtypeStruct((ROWS, WIDTH), jnp.bfloat16),
                jax.ShapeDtypeStruct((16 * ROWS, 256), jnp.bfloat16),
            ),
            scalars,
            report_proj,
            caption_mine,
            caption_received,
        )
    with jax.named_scope("report_relay_near"):
        report_2a = moved_by(report_1[:64], 2)
    with jax.named_scope("report_relay_far"):
        report_2b = moved_by(report_3[64:], -2)
    with jax.named_scope("report_beside"):
        report_beside = beside(report_late, 1, 8)
    with jax.named_scope("picture_kernel"):
        picture_mine, picture_theirs = window_call(
            picture_kernel,
            PICTURE_FLOPS,
            scalars,
            place,
            pair_index.reshape(ROWS, 1),
            image_proj,
            image_other,
            report_proj,
            report_1,
            report_2a,
            report_2b,
            report_3,
            report_beside,
        )
    with jax.named_scope("picture_swap"):
        picture_received = swapped(picture_theirs)
    with jax.named_scope("picture_finish"):
        (picture_grad,) = finish_call(
            (jax.ShapeDtypeStruct((ROWS, WIDTH), jnp.bfloat16),),
            scalars,
            image_proj,
            picture_mine,
            picture_received,
        )

    with jax.named_scope("captions"):
        caps = lax.all_to_all(
            after(caption_spread, feats),
            ("x", "y"),
            split_axis=0,
            concat_axis=0,
            tiled=True,
        )
    with jax.named_scope("head_kernel"):
        keep, give = head_call(place, after(caps, report_2a, report_2b, report_beside), feats)
    with jax.named_scope("head_swap"):
        part = (keep + swapped(give)).astype(jnp.bfloat16)
    with jax.named_scope("head_sum"):
        parts = lax.all_to_all(part, ("zl", "zh", "y"), split_axis=0, concat_axis=0, tiled=True)
        head = jnp.sum(parts.reshape(16, 4, 8, 256).astype(jnp.float32), axis=0)
        head_grad = head.transpose(1, 0, 2).reshape(8, WIDTH)
    return (picture_grad, caption_grad, head_grad)


def solution(mesh):
    fine = Mesh(mesh.devices.reshape(4, 4, 4, 4, 2), AXES)
    rows = P(AXES, None)
    return jax.shard_map(
        on_device,
        mesh=fine,
        in_specs=(rows, rows, rows, P(AXES), P(), P()),
        out_specs=(rows, rows, rows),
        check_vma=False,
    )
```

```python
import jax
import jax.numpy as jnp
from jax import lax
from jax.experimental import pallas as pl
from jax.experimental.pallas import tpu as pltpu
from jax.sharding import Mesh, PartitionSpec as P

EPSILON = 1e-06
ROWS = 128
WIDTH = 1024
BLOCKS = 512
AXES = ("zl", "x", "y", "zh", "c")
LIMIT = 40 * 1024 * 1024
WINDOW_FLOPS = 4 * ROWS * 8 * ROWS * WIDTH
CAPTION_FLOPS = 61 * WINDOW_FLOPS
READY_FLOPS = 20 * WINDOW_FLOPS
PICTURE_FLOPS = 1 * WINDOW_FLOPS
HEAD_FLOPS = 2 * 2048 * 1024 * 256


def moved(value, target_of):
    return lax.ppermute(value, AXES, [(r, target_of(r) % BLOCKS) for r in range(BLOCKS)])


def moved_by(value, steps):
    return moved(value, lambda r: r + steps)


def swapped(value):
    return lax.ppermute(value, "c", [(0, 1), (1, 0)])


def beside(value, parity, steps):
    pairs = [(r, (r + steps) % BLOCKS) for r in range(parity, BLOCKS, 2)]
    return lax.ppermute(value, AXES, pairs)


def after(value, *others):
    return lax.optimization_barrier((value, *others))[0]


def low_rows(wide):
    inverse = 1.0 / jnp.sqrt(jnp.sum(wide * wide, axis=-1, keepdims=True) + EPSILON)
    return (wide * inverse).astype(jnp.bfloat16)


def unit_rows(own):
    wide = own[...].astype(jnp.float32)
    length = jnp.sqrt(jnp.sum(wide * wide, axis=-1, keepdims=True) + EPSILON)
    return wide / length, length


def slopes(scalars, rows, blocks):
    logits = lax.dot_general(
        rows.astype(jnp.bfloat16), blocks, (((1,), (1,)), ((), ())), preferred_element_type=jnp.float32
    )
    return scalars[0] * logits + scalars[1]


def window_sums(scalars, match, use_beside, own, other, blocks, beside, mine, theirs, low):
    start = 0
    for ref in blocks:
        rows = ref.shape[0]
        low[start : start + rows, :] = low_rows(ref[...].astype(jnp.float32))
        start += rows
    last = jnp.where(use_beside, beside[...].astype(jnp.float32), blocks[0][...].astype(jnp.float32))
    low[start : start + ROWS, :] = low_rows(last)
    unit, _ = unit_rows(own)
    logits = slopes(scalars, unit, low[:512, :])
    target = jnp.where(match, 1.0, -1.0)
    first = -target * jax.nn.sigmoid(-target * logits[:, :ROWS])
    slope = jnp.concatenate([first, jax.nn.sigmoid(logits[:, ROWS:])], axis=1)
    mine[...] = jnp.dot(
        slope.astype(jnp.bfloat16), low[:512, :], preferred_element_type=jnp.float32
    )
    unit, _ = unit_rows(other)
    slope = jax.nn.sigmoid(slopes(scalars, unit, low[ROWS:, :]))
    theirs[...] = jnp.dot(
        slope.astype(jnp.bfloat16), low[ROWS:, :], preferred_element_type=jnp.float32
    )


def caption_kernel(scalars, place, pair_row, own, other, *refs):
    *blocks, beside, mine, theirs, low = refs
    rows = lax.broadcasted_iota(jnp.int32, (ROWS, ROWS), 0)
    match = rows == lax.rem(pair_row[...], ROWS)
    window_sums(scalars, match, place[0] == 0, own, other, blocks, beside, mine, theirs, low)


def picture_kernel(scalars, place, pair_column, own, other, *refs):
    *blocks, beside, mine, theirs, low = refs
    columns = lax.broadcasted_iota(jnp.int32, (ROWS, ROWS), 1)
    match = columns == lax.rem(pair_column[...], ROWS)
    window_sums(scalars, match, place[0] == 1, own, other, blocks, beside, mine, theirs, low)


def window_call(body, flops, *args):
    vmem = pl.BlockSpec(memory_space=pltpu.VMEM)
    half = jax.ShapeDtypeStruct((ROWS, WIDTH), jnp.float32)
    return pl.pallas_call(
        body,
        out_shape=(half, half),
        in_specs=[pl.BlockSpec(memory_space=pltpu.SMEM)] * 2 + [vmem] * (len(args) - 2),
        out_specs=(vmem, vmem),
        scratch_shapes=[pltpu.VMEM((5 * ROWS, WIDTH), jnp.bfloat16)],
        compiler_params=pltpu.CompilerParams(vmem_limit_bytes=LIMIT),
        cost_estimate=pl.CostEstimate(
            flops=flops, bytes_accessed=4_000_000, transcendentals=ROWS * 1024
        ),
    )(*args)


def finish_kernel(scalars, own, mine, received, out, *spread):
    unit, length = unit_rows(own)
    total = scalars[0] * (mine[...] + received[...])
    grad = (total - unit * jnp.sum(unit * total, axis=-1, keepdims=True)) / length
    grad = grad.astype(jnp.bfloat16)
    out[...] = grad
    for ref in spread:
        for x in range(4):
            for y in range(4):
                row = (x * 4 + y) * ROWS
                ref[row : row + ROWS, :] = grad[:, y * 256 : (y + 1) * 256]


def finish_call(outs, *args):
    vmem = pl.BlockSpec(memory_space=pltpu.VMEM)
    return pl.pallas_call(
        finish_kernel,
        out_shape=outs,
        in_specs=[pl.BlockSpec(memory_space=pltpu.SMEM)] + [vmem] * 3,
        out_specs=tuple([vmem] * len(outs)),
        compiler_params=pltpu.CompilerParams(vmem_limit_bytes=LIMIT),
        cost_estimate=pl.CostEstimate(flops=0, bytes_accessed=1_500_000, transcendentals=0),
    )(*args)


def head_kernel(place, caps, feats, arrived, keep, give, table):
    c = place[0]
    total = lax.dot_general(
        caps[...], feats[...], (((0,), (0,)), ((), ())), preferred_element_type=jnp.float32
    )
    table[...] = total.T
    for zl in range(4):
        for zh in range(4):
            for y in range(4):
                base = zl * 256 + y * 64 + zh * 16
                to = (zl * 16 + zh * 4 + y) * 8
                keep[to : to + 8, :] = table[pl.ds(pl.multiple_of(base + c * 8, 8), 8), :]
                give[to : to + 8, :] = table[pl.ds(pl.multiple_of(base + 8 - c * 8, 8), 8), :]


def head_call(place, caps, feats, arrived):
    vmem = pl.BlockSpec(memory_space=pltpu.VMEM)
    half = jax.ShapeDtypeStruct((512, 256), jnp.float32)
    return pl.pallas_call(
        head_kernel,
        out_shape=(half, half),
        in_specs=[pl.BlockSpec(memory_space=pltpu.SMEM)] + [vmem] * 3,
        out_specs=(vmem, vmem),
        scratch_shapes=[pltpu.VMEM((1024, 256), jnp.float32)],
        compiler_params=pltpu.CompilerParams(vmem_limit_bytes=LIMIT),
        cost_estimate=pl.CostEstimate(
            flops=HEAD_FLOPS, bytes_accessed=6_000_000, transcendentals=0
        ),
    )(place, caps, feats, arrived)


def ready_kernel(first, out):
    out[...] = first[...].astype(jnp.float32)


def ready(first):
    return pl.pallas_call(
        ready_kernel,
        grid=(1,),
        out_shape=jax.ShapeDtypeStruct((16, 128), jnp.float32),
        in_specs=[pl.BlockSpec((16, 128), lambda i: (0, 0))],
        out_specs=pl.BlockSpec((16, 128), lambda i: (0, 0)),
        cost_estimate=pl.CostEstimate(flops=READY_FLOPS, bytes_accessed=16384, transcendentals=0),
    )(first)


def columns_kernel(feats, out):
    for x in range(4):
        for zl in range(4):
            piece = feats[:, zl * 1024 + x * 256 : zl * 1024 + x * 256 + 256]
            for y in range(4):
                row = (x * 4 + y) * ROWS
                out[row : row + ROWS, zl * 256 : zl * 256 + 256] = piece


def columns_call(feats):
    vmem = pl.BlockSpec(memory_space=pltpu.VMEM)
    return pl.pallas_call(
        columns_kernel,
        out_shape=jax.ShapeDtypeStruct((16 * ROWS, WIDTH), jnp.bfloat16),
        in_specs=[vmem],
        out_specs=vmem,
        compiler_params=pltpu.CompilerParams(vmem_limit_bytes=LIMIT),
        cost_estimate=pl.CostEstimate(flops=0, bytes_accessed=5_000_000, transcendentals=0),
    )(feats)


def on_device(image_proj, report_proj, report_feats, pair_index, natural_log_factor, logit_bias):
    scalars = jnp.concatenate([jnp.exp(natural_log_factor), logit_bias])
    place = lax.axis_index("c").astype(jnp.int32).reshape(1)

    with jax.named_scope("image_near"):
        image_1 = moved_by(image_proj, -2)
    with jax.named_scope("image_far"):
        image_3 = moved_by(image_proj, -6)
    with jax.named_scope("image_beside"):
        image_beside = beside(image_proj, 0, -8)
    with jax.named_scope("core_swap"):
        report_other = swapped(report_proj)

    with jax.named_scope("feats"):
        feats = lax.all_to_all(
            columns_call(after(report_feats, image_beside)), ("x", "y"), split_axis=0, concat_axis=0, tiled=True
        )

    with jax.named_scope("image_relay_near"):
        image_2a = moved_by(image_1[:64], -2)
    with jax.named_scope("image_relay_far"):
        image_2b = moved_by(image_3[64:], 2)
    with jax.named_scope("caption_kernel"):
        caption_mine, caption_theirs = window_call(
            caption_kernel,
            CAPTION_FLOPS,
            scalars,
            place,
            pair_index.reshape(1, ROWS),
            report_proj,
            report_other,
            image_proj,
            image_1,
            image_2a,
            image_2b,
            image_3,
            image_beside,
        )
    report_late = after(report_proj, image_1, image_3)
    with jax.named_scope("report_near"):
        report_1 = moved_by(report_late, 2)
    with jax.named_scope("report_far"):
        report_3 = moved_by(report_late, 6)
    with jax.named_scope("caption_swap"):
        caption_received = swapped(after(caption_theirs, report_1, report_3))
    with jax.named_scope("caption_finish"):
        caption_grad, caption_spread = finish_call(
            (
                jax.ShapeDtypeStruct((ROWS, WIDTH), jnp.bfloat16),
                jax.ShapeDtypeStruct((16 * ROWS, 256), jnp.bfloat16),
            ),
            scalars,
            report_proj,
            caption_mine,
            caption_received,
        )
    with jax.named_scope("report_relay"):
        report_2 = moved_by(report_1, 2)
    with jax.named_scope("report_beside"):
        report_beside = beside(after(report_late, caption_grad), 1, 8)
    with jax.named_scope("image_swap"):
        image_other = swapped(after(image_proj, caption_grad))
    with jax.named_scope("picture_kernel"):
        picture_mine, picture_theirs = window_call(
            picture_kernel,
            PICTURE_FLOPS,
            scalars,
            place,
            pair_index.reshape(ROWS, 1),
            image_proj,
            image_other,
            report_proj,
            report_1,
            report_2,
            report_3,
            report_beside,
        )
    with jax.named_scope("picture_swap"):
        picture_received = swapped(picture_theirs)
    with jax.named_scope("picture_finish"):
        (picture_grad,) = finish_call(
            (jax.ShapeDtypeStruct((ROWS, WIDTH), jnp.bfloat16),),
            scalars,
            image_proj,
            picture_mine,
            picture_received,
        )

    with jax.named_scope("captions"):
        caps = lax.all_to_all(
            after(caption_spread, feats),
            ("x", "y"),
            split_axis=0,
            concat_axis=0,
            tiled=True,
        )
    with jax.named_scope("head_kernel"):
        keep, give = head_call(place, after(caps, report_beside), feats, ready(report_2))
    with jax.named_scope("head_swap"):
        part = (keep + swapped(give)).astype(jnp.bfloat16)
    with jax.named_scope("head_sum"):
        parts = lax.all_to_all(part, ("zl", "zh", "y"), split_axis=0, concat_axis=0, tiled=True)
        head = jnp.sum(parts.reshape(16, 4, 8, 256).astype(jnp.float32), axis=0)
        head_grad = head.transpose(1, 0, 2).reshape(8, WIDTH)
    return (picture_grad, caption_grad, head_grad)


def solution(mesh):
    fine = Mesh(mesh.devices.reshape(4, 4, 4, 4, 2), AXES)
    rows = P(AXES, None)
    return jax.shard_map(
        on_device,
        mesh=fine,
        in_specs=(rows, rows, rows, P(AXES), P(), P()),
        out_specs=(rows, rows, rows),
        check_vma=False,
    )
```

```python
import jax
import jax.numpy as jnp
from jax import lax
from jax.experimental import pallas as pl
from jax.experimental.pallas import tpu as pltpu
from jax.sharding import Mesh, PartitionSpec as P

EPSILON = 1e-06
ROWS = 128
WIDTH = 1024
BLOCKS = 512
AXES = ("zl", "x", "y", "zh", "c")
LIMIT = 40 * 1024 * 1024
WINDOW_FLOPS = 4 * ROWS * 8 * ROWS * WIDTH
CAPTION_FLOPS = 61 * WINDOW_FLOPS
READY_FLOPS = 20 * WINDOW_FLOPS
PICTURE_FLOPS = 1 * WINDOW_FLOPS
HEAD_FLOPS = 2 * 2048 * 1024 * 256


def moved(value, target_of):
    return lax.ppermute(value, AXES, [(r, target_of(r) % BLOCKS) for r in range(BLOCKS)])


def moved_by(value, steps):
    return moved(value, lambda r: r + steps)


def swapped(value):
    return lax.ppermute(value, "c", [(0, 1), (1, 0)])


def beside(value, parity, steps):
    pairs = [(r, (r + steps) % BLOCKS) for r in range(parity, BLOCKS, 2)]
    return lax.ppermute(value, AXES, pairs)


def after(value, *others):
    return lax.optimization_barrier((value, *others))[0]


def low_rows(wide):
    inverse = 1.0 / jnp.sqrt(jnp.sum(wide * wide, axis=-1, keepdims=True) + EPSILON)
    return (wide * inverse).astype(jnp.bfloat16)


def unit_rows(own):
    wide = own[...].astype(jnp.float32)
    length = jnp.sqrt(jnp.sum(wide * wide, axis=-1, keepdims=True) + EPSILON)
    return wide / length, length


def slopes(scalars, rows, blocks):
    logits = lax.dot_general(
        rows.astype(jnp.bfloat16), blocks, (((1,), (1,)), ((), ())), preferred_element_type=jnp.float32
    )
    return scalars[0] * logits + scalars[1]


def window_sums(scalars, match, use_beside, own, other, blocks, beside, mine, theirs, low):
    start = 0
    for ref in blocks:
        rows = ref.shape[0]
        low[start : start + rows, :] = low_rows(ref[...].astype(jnp.float32))
        start += rows
    last = jnp.where(use_beside, beside[...].astype(jnp.float32), blocks[0][...].astype(jnp.float32))
    low[start : start + ROWS, :] = low_rows(last)
    unit, _ = unit_rows(own)
    logits = slopes(scalars, unit, low[:512, :])
    target = jnp.where(match, 1.0, -1.0)
    first = -target * jax.nn.sigmoid(-target * logits[:, :ROWS])
    slope = jnp.concatenate([first, jax.nn.sigmoid(logits[:, ROWS:])], axis=1)
    mine[...] = jnp.dot(
        slope.astype(jnp.bfloat16), low[:512, :], preferred_element_type=jnp.float32
    )
    unit, _ = unit_rows(other)
    slope = jax.nn.sigmoid(slopes(scalars, unit, low[ROWS:, :]))
    theirs[...] = jnp.dot(
        slope.astype(jnp.bfloat16), low[ROWS:, :], preferred_element_type=jnp.float32
    )


def caption_kernel(scalars, place, pair_row, own, other, *refs):
    *blocks, beside, mine, theirs, low = refs
    rows = lax.broadcasted_iota(jnp.int32, (ROWS, ROWS), 0)
    match = rows == lax.rem(pair_row[...], ROWS)
    window_sums(scalars, match, place[0] == 0, own, other, blocks, beside, mine, theirs, low)


def picture_kernel(scalars, place, pair_column, own, other, *refs):
    *blocks, beside, mine, theirs, low = refs
    columns = lax.broadcasted_iota(jnp.int32, (ROWS, ROWS), 1)
    match = columns == lax.rem(pair_column[...], ROWS)
    window_sums(scalars, match, place[0] == 1, own, other, blocks, beside, mine, theirs, low)


def window_call(body, flops, *args):
    vmem = pl.BlockSpec(memory_space=pltpu.VMEM)
    half = jax.ShapeDtypeStruct((ROWS, WIDTH), jnp.float32)
    return pl.pallas_call(
        body,
        out_shape=(half, half),
        in_specs=[pl.BlockSpec(memory_space=pltpu.SMEM)] * 2 + [vmem] * (len(args) - 2),
        out_specs=(vmem, vmem),
        scratch_shapes=[pltpu.VMEM((5 * ROWS, WIDTH), jnp.bfloat16)],
        compiler_params=pltpu.CompilerParams(vmem_limit_bytes=LIMIT),
        cost_estimate=pl.CostEstimate(
            flops=flops, bytes_accessed=4_000_000, transcendentals=ROWS * 1024
        ),
    )(*args)


def finish_kernel(scalars, own, mine, received, out, *spread):
    unit, length = unit_rows(own)
    total = scalars[0] * (mine[...] + received[...])
    grad = (total - unit * jnp.sum(unit * total, axis=-1, keepdims=True)) / length
    grad = grad.astype(jnp.bfloat16)
    out[...] = grad
    for ref in spread:
        for x in range(4):
            for y in range(4):
                row = (x * 4 + y) * ROWS
                ref[row : row + ROWS, :] = grad[:, y * 256 : (y + 1) * 256]


def finish_call(outs, *args):
    vmem = pl.BlockSpec(memory_space=pltpu.VMEM)
    return pl.pallas_call(
        finish_kernel,
        out_shape=outs,
        in_specs=[pl.BlockSpec(memory_space=pltpu.SMEM)] + [vmem] * 3,
        out_specs=tuple([vmem] * len(outs)),
        compiler_params=pltpu.CompilerParams(vmem_limit_bytes=LIMIT),
        cost_estimate=pl.CostEstimate(flops=0, bytes_accessed=1_500_000, transcendentals=0),
    )(*args)


def head_kernel(place, caps, feats, arrived, keep, give, table):
    c = place[0]
    total = lax.dot_general(
        caps[...], feats[...], (((0,), (0,)), ((), ())), preferred_element_type=jnp.float32
    )
    table[...] = total.T
    for zl in range(4):
        for zh in range(4):
            for y in range(4):
                base = zl * 256 + y * 64 + zh * 16
                to = (zl * 16 + zh * 4 + y) * 8
                keep[to : to + 8, :] = table[pl.ds(pl.multiple_of(base + c * 8, 8), 8), :]
                give[to : to + 8, :] = table[pl.ds(pl.multiple_of(base + 8 - c * 8, 8), 8), :]


def head_call(place, caps, feats, arrived):
    vmem = pl.BlockSpec(memory_space=pltpu.VMEM)
    half = jax.ShapeDtypeStruct((512, 256), jnp.float32)
    return pl.pallas_call(
        head_kernel,
        out_shape=(half, half),
        in_specs=[pl.BlockSpec(memory_space=pltpu.SMEM)] + [vmem] * 3,
        out_specs=(vmem, vmem),
        scratch_shapes=[pltpu.VMEM((1024, 256), jnp.float32)],
        compiler_params=pltpu.CompilerParams(vmem_limit_bytes=LIMIT),
        cost_estimate=pl.CostEstimate(
            flops=HEAD_FLOPS, bytes_accessed=6_000_000, transcendentals=0
        ),
    )(place, caps, feats, arrived)


def ready_kernel(first, out):
    out[...] = first[...].astype(jnp.float32)


def ready(first):
    return pl.pallas_call(
        ready_kernel,
        grid=(1,),
        out_shape=jax.ShapeDtypeStruct((16, 128), jnp.float32),
        in_specs=[pl.BlockSpec((16, 128), lambda i: (0, 0))],
        out_specs=pl.BlockSpec((16, 128), lambda i: (0, 0)),
        cost_estimate=pl.CostEstimate(flops=READY_FLOPS, bytes_accessed=16384, transcendentals=0),
    )(first)


def columns_kernel(feats, out, held, sems):
    copy = pltpu.make_async_copy(feats, held, sems.at[64])
    copy.start()
    copy.wait()
    copies = []
    for x in range(4):
        for zl in range(4):
            for y in range(4):
                row = (x * 4 + y) * ROWS
                copies.append(
                    pltpu.make_async_copy(
                        held.at[:, pl.ds(zl * 1024 + x * 256, 256)],
                        out.at[pl.ds(row, ROWS), pl.ds(zl * 256, 256)],
                        sems.at[(x * 4 + zl) * 4 + y],
                    )
                )
    for copy in copies:
        copy.start()
    for copy in copies:
        copy.wait()


def columns_call(feats):
    anywhere = pl.BlockSpec(memory_space=pl.ANY)
    return pl.pallas_call(
        columns_kernel,
        out_shape=jax.ShapeDtypeStruct((16 * ROWS, WIDTH), jnp.bfloat16),
        in_specs=[anywhere],
        out_specs=anywhere,
        scratch_shapes=[
            pltpu.VMEM((ROWS, 4 * WIDTH), jnp.bfloat16),
            pltpu.SemaphoreType.DMA((65,)),
        ],
        compiler_params=pltpu.CompilerParams(vmem_limit_bytes=LIMIT),
        cost_estimate=pl.CostEstimate(flops=0, bytes_accessed=5_000_000, transcendentals=0),
    )(feats)


def on_device(image_proj, report_proj, report_feats, pair_index, natural_log_factor, logit_bias):
    scalars = jnp.concatenate([jnp.exp(natural_log_factor), logit_bias])
    place = lax.axis_index("c").astype(jnp.int32).reshape(1)

    with jax.named_scope("image_near"):
        image_1 = moved_by(image_proj, -2)
    with jax.named_scope("image_far"):
        image_3 = moved_by(image_proj, -6)
    with jax.named_scope("image_beside"):
        image_beside = beside(image_proj, 0, -8)
    with jax.named_scope("core_swap"):
        report_other = swapped(report_proj)

    with jax.named_scope("feats"):
        feats = lax.all_to_all(
            columns_call(after(report_feats, image_beside)), ("x", "y"), split_axis=0, concat_axis=0, tiled=True
        )

    with jax.named_scope("image_relay_near"):
        image_2a = moved_by(image_1[:64], -2)
    with jax.named_scope("image_relay_far"):
        image_2b = moved_by(image_3[64:], 2)
    with jax.named_scope("caption_kernel"):
        caption_mine, caption_theirs = window_call(
            caption_kernel,
            CAPTION_FLOPS,
            scalars,
            place,
            pair_index.reshape(1, ROWS),
            report_proj,
            report_other,
            image_proj,
            image_1,
            image_2a,
            image_2b,
            image_3,
            image_beside,
        )
    report_late = after(report_proj, image_1, image_3)
    with jax.named_scope("report_near"):
        report_1 = moved_by(report_late, 2)
    with jax.named_scope("report_far"):
        report_3 = moved_by(report_late, 6)
    with jax.named_scope("caption_swap"):
        caption_received = swapped(after(caption_theirs, report_1, report_3))
    with jax.named_scope("caption_finish"):
        caption_grad, caption_spread = finish_call(
            (
                jax.ShapeDtypeStruct((ROWS, WIDTH), jnp.bfloat16),
                jax.ShapeDtypeStruct((16 * ROWS, 256), jnp.bfloat16),
            ),
            scalars,
            report_proj,
            caption_mine,
            caption_received,
        )
    with jax.named_scope("report_relay"):
        report_2 = moved_by(report_1, 2)
    with jax.named_scope("report_beside"):
        report_beside = beside(after(report_late, caption_grad), 1, 8)
    with jax.named_scope("image_swap"):
        image_other = swapped(after(image_proj, caption_grad))
    with jax.named_scope("picture_kernel"):
        picture_mine, picture_theirs = window_call(
            picture_kernel,
            PICTURE_FLOPS,
            scalars,
            place,
            pair_index.reshape(ROWS, 1),
            image_proj,
            image_other,
            report_proj,
            report_1,
            report_2,
            report_3,
            report_beside,
        )
    with jax.named_scope("picture_swap"):
        picture_received = swapped(picture_theirs)
    with jax.named_scope("picture_finish"):
        (picture_grad,) = finish_call(
            (jax.ShapeDtypeStruct((ROWS, WIDTH), jnp.bfloat16),),
            scalars,
            image_proj,
            picture_mine,
            picture_received,
        )

    with jax.named_scope("captions"):
        caps = lax.all_to_all(
            after(caption_spread, feats),
            ("x", "y"),
            split_axis=0,
            concat_axis=0,
            tiled=True,
        )
    with jax.named_scope("head_kernel"):
        keep, give = head_call(place, after(caps, report_beside), feats, ready(report_2))
    with jax.named_scope("head_swap"):
        part = (keep + swapped(give)).astype(jnp.bfloat16)
    with jax.named_scope("head_sum"):
        parts = lax.all_to_all(part, ("zl", "zh", "y"), split_axis=0, concat_axis=0, tiled=True)
        head = jnp.sum(parts.reshape(16, 4, 8, 256).astype(jnp.float32), axis=0)
        head_grad = head.transpose(1, 0, 2).reshape(8, WIDTH)
    return (picture_grad, caption_grad, head_grad)


def solution(mesh):
    fine = Mesh(mesh.devices.reshape(4, 4, 4, 4, 2), AXES)
    rows = P(AXES, None)
    return jax.shard_map(
        on_device,
        mesh=fine,
        in_specs=(rows, rows, rows, P(AXES), P(), P()),
        out_specs=(rows, rows, rows),
        check_vma=False,
    )
```
